32 devices in a mesh: morton: 8 (over z, x), slab: 4 (over y, core).
Axes of the slice: x: 2, y: 2, z: 4, core: 2. Of those that a mesh axis runs over, the one named last changes fastest.
Arguments:
- multipole: bfloat16 [3, 488, 8192], P(None, None, ('morton', 'slab')), may hold values from -1.796875 to 1.796875
- positions: bfloat16 [3, 128, 8192], P(None, None, ('morton', 'slab')), may hold values from 0 to 1
- strengths: bfloat16 [3, 128, 8192], P(None, None, ('morton', 'slab')), may hold values from -3 to 3
- vlist: int32 [27, 8192], P(None, ('morton', 'slab')), may hold values from -1 to 48, as said below
- ulist: int32 [9, 8192], P(None, ('morton', 'slab')), may hold values from -1 to 8, as said below
Outputs:
- check: float32 [3, 488, 8192], P(None, None, ('morton', 'slab'))
- potential: float32 [3, 128, 8192], P(None, None, ('morton', 'slab'))
The draws below stay inside these ranges and needn't reach their ends.
Inputs may be any that keep to these rules, and one draw needn't show every extreme that they name: `vlist`: entry k of leaf t is -1 or the code 7 * (dx + 3) + (dy + 3) of the k-th offset, in increasing code, of the leaf's pattern: the offsets with dx from -2 - (x_t % 2) to 3 - (x_t % 2) and dy from -2 - (y_t % 2) to 3 - (y_t % 2), except those with |dx| <= 1 and |dy| <= 1. It is -1 exactly where the leaf (x_t + dx, y_t + dy) lies outside the grid or one of the two leaves is unoccupied; occupancy is the same as in ulist. `ulist`: entry k of leaf t is -1 or k, naming the offset dx = k // 3 - 1, dy = k % 3 - 1; it is -1 exactly where that leaf lies outside the grid or one of the two leaves is unoccupied.
All inputs are finite; a program needn't handle non-finite values.
Results may differ from the reference program's by a relative error of at most 0.003.
Values may be sent and summed in bfloat16 or wider, within the bound.
A program may use at most 128 MiB of HBM per device.

```python
import math
import jax
import jax.numpy as jnp
import numpy as np
from jax import lax

SIDE = 16
P_SIZE = 128
EQ_SIDE = 10
Q = 488
GRID_X = 256
GRID_Y = 32
LEAVES = 8192
N_MORTON = 8


def pattern_tables():
    table_x = np.zeros((2, 2, 27), np.int32)
    table_y = np.zeros((2, 2, 27), np.int32)
    for parity_y in (0, 1):
        for parity_x in (0, 1):
            entry = 0
            for shift_x in range(-2 - parity_x, 4 - parity_x):
                for shift_y in range(-2 - parity_y, 4 - parity_y):
                    if abs(shift_x) > 1 or abs(shift_y) > 1:
                        table_x[parity_y, parity_x, entry] = shift_x
                        table_y[parity_y, parity_x, entry] = shift_y
                        entry = entry + 1
    return (table_x, table_y)


def leaf_order(values):
    tiles = GRID_X // (2 * SIDE)
    count = values.shape[0]
    shaped = values.reshape((count, 2, SIDE, tiles, 2, SIDE))
    return shaped.transpose(0, 3, 1, 4, 2, 5).reshape((count, GRID_X * GRID_Y))


def occupancy(key):
    tiles = GRID_X // (2 * SIDE)
    fill_level = jax.random.randint(jax.random.fold_in(key, 12), (tiles,), 3, 9)
    column_level = jnp.repeat(fill_level, 2 * SIDE)
    draws_int = jax.random.randint(jax.random.fold_in(key, 11), (GRID_Y, GRID_X), 0, 8)
    return (draws_int < column_level[None, :]).astype(jnp.int32)


def offset_codes(key, shifts_x, shifts_y, codes):
    occupied = occupancy(key)
    padded = jnp.pad(occupied, 3)
    rows_y = jnp.arange(GRID_Y, dtype=jnp.int32)[:, None] + jnp.zeros((1, GRID_X), jnp.int32)
    cols_x = jnp.arange(GRID_X, dtype=jnp.int32)[None, :] + jnp.zeros((GRID_Y, 1), jnp.int32)
    listed = []
    for entry in range(len(codes)):
        step_x = shifts_x[entry]
        step_y = shifts_y[entry]
        source_y = rows_y + step_y
        source_x = cols_x + step_x
        inside = (source_y >= 0) & (source_y < GRID_Y) & (source_x >= 0) & (source_x < GRID_X)
        source_occupied = padded[source_y + 3, source_x + 3]
        present = inside & (source_occupied == 1) & (occupied == 1)
        listed.append(jnp.where(present, codes[entry], -1))
    return leaf_order(jnp.stack(listed)).astype(jnp.int32)


def draw_vlist(key, part):
    table_x, table_y = pattern_tables()
    parity_y = jnp.arange(GRID_Y, dtype=jnp.int32)[:, None] % 2 + jnp.zeros((1, GRID_X), jnp.int32)
    parity_x = jnp.arange(GRID_X, dtype=jnp.int32)[None, :] % 2 + jnp.zeros((GRID_Y, 1), jnp.int32)
    shifts_x = []
    shifts_y = []
    codes = []
    for entry in range(27):
        step_x = jnp.asarray(table_x[:, :, entry])[parity_y, parity_x]
        step_y = jnp.asarray(table_y[:, :, entry])[parity_y, parity_x]
        shifts_x.append(step_x)
        shifts_y.append(step_y)
        codes.append(7 * (step_x + 3) + (step_y + 3))
    return offset_codes(key, shifts_x, shifts_y, codes)


def draw_ulist(key, part):
    shifts_x = []
    shifts_y = []
    codes = []
    for entry in range(9):
        shifts_x.append(entry // 3 - 1)
        shifts_y.append(entry % 3 - 1)
        codes.append(entry)
    return offset_codes(key, shifts_x, shifts_y, codes)


def steps_of(key, shape, cuts, smallest, largest):
    factor_of = 1.0
    for dim, parts in cuts:
        heights = jax.random.uniform(jax.random.fold_in(jax.random.fold_in(key, 6), dim), (parts,), jnp.float32, smallest / len(cuts), largest / len(cuts))
        factor_of = factor_of * jnp.repeat(jnp.exp(heights), shape[dim] // parts).reshape((-1,) + (1,) * (len(shape) - 1 - dim))
    return factor_of


def centred(key, shape, deviation, most, shards=(), kind=jnp.bfloat16):
    drawn = deviation * jax.random.normal(key, shape, jnp.float32)
    if shards:
        drawn = drawn * steps_of(key, shape, shards, -0.22, 0.18)
    return jnp.clip(drawn, -most, most).astype(kind)


def setup_inputs(seed: int = 0) -> dict:
    splits = jax.random.split(jax.random.key(seed), 6)
    multipole = centred(splits[0], (3, Q, LEAVES), 0.3, 1.796875, ((2, 32),))
    positions = jnp.clip(1.0 * jax.random.uniform(splits[1], (3, P_SIZE, LEAVES), jnp.float32) ** steps_of(splits[1], (3, P_SIZE, LEAVES), ((2, 32),), -0.2, 0.2), 0.0, 1.0).astype(jnp.bfloat16)
    strengths = centred(splits[2], (3, P_SIZE, LEAVES), 0.5, 3.0, ((2, 32),))
    vlist = draw_vlist(jax.random.fold_in(splits[5], 71), 0)
    ulist = draw_ulist(jax.random.fold_in(splits[5], 71), 0)
    return {"multipole": multipole, "positions": positions, "strengths": strengths, "vlist": vlist, "ulist": ulist}


FOUR_PI = 4.0 * math.pi
DELTA_SQ = 0.01
RADIUS = 0.525

def surface_points(per_edge):
    grid_line = np.linspace(-1.0, 1.0, per_edge)
    first, second, third = np.meshgrid(grid_line, grid_line, grid_line, indexing='ij')
    stacked = np.stack([first.ravel(), second.ravel(), third.ravel()], axis=1)
    on_face = np.max(np.abs(stacked), axis=1) > 0.999
    return (stacked[on_face] * RADIUS).astype(np.float32)

def class_offsets(parity_x, parity_y):
    listed = []
    for shift_x in range(-2 - parity_x, 4 - parity_x):
        for shift_y in range(-2 - parity_y, 4 - parity_y):
            if abs(shift_x) > 1 or abs(shift_y) > 1:
                listed.append((shift_x, shift_y))
    return listed

def translation(shift_x, shift_y):
    points = jnp.asarray(surface_points(EQ_SIDE))
    delta_x = points[:, None, 0] - points[None, :, 0] - shift_x
    delta_y = points[:, None, 1] - points[None, :, 1] - shift_y
    delta_z = points[:, None, 2] - points[None, :, 2]
    distance = jnp.sqrt(delta_x * delta_x + delta_y * delta_y + delta_z * delta_z)
    return (1.0 / (FOUR_PI * distance)).astype(jnp.bfloat16)

def to_grid(values):
    leading = values.shape[:-1]
    count = len(leading)
    shaped = values.reshape(leading + (N_MORTON, 2, 2, SIDE, SIDE))
    order = tuple(range(count)) + (count + 1, count + 3, count, count + 2, count + 4)
    return shaped.transpose(order).reshape(leading + (2 * SIDE, 2 * SIDE * N_MORTON))

def from_grid(values):
    leading = values.shape[:-2]
    count = len(leading)
    shaped = values.reshape(leading + (2, SIDE, N_MORTON, 2, SIDE))
    order = tuple(range(count)) + (count + 2, count, count + 3, count + 1, count + 4)
    return shaped.transpose(order).reshape(leading + (LEAVES,))

def far_field(multipole, vlist):
    grid_y = 2 * SIDE
    grid_x = 2 * SIDE * N_MORTON
    padded = jnp.pad(to_grid(multipole), ((0, 0), (0, 0), (3, 3), (3, 3)))
    lists = to_grid(vlist)
    result = jnp.zeros((3, Q, grid_y, grid_x), jnp.float32)
    for parity_y in (0, 1):
        for parity_x in (0, 1):
            partial_sum = jnp.zeros((3, Q, grid_y // 2, grid_x // 2), jnp.float32)
            for entry, (shift_x, shift_y) in enumerate(class_offsets(parity_x, parity_y)):
                top = 3 + parity_y + shift_y
                left = 3 + parity_x + shift_x
                source = padded[:, :, top:top + grid_y:2, left:left + grid_x:2]
                offset_code = 7 * (shift_x + 3) + (shift_y + 3)
                live_mask = (lists[entry, parity_y::2, parity_x::2] == offset_code).astype(source.dtype)
                source = (source * live_mask).astype(jnp.float32)
                kernel_table = translation(shift_x, shift_y).astype(jnp.float32)
                partial_sum = partial_sum + jnp.einsum('ij,cjab->ciab', kernel_table, source, precision=lax.Precision.HIGHEST)
            result = result.at[:, :, parity_y::2, parity_x::2].set(partial_sum)
    return from_grid(result)

def row_potential(place, weight, lists, width, leaf_row):
    target = lax.dynamic_slice_in_dim(place, leaf_row + 1, 1, 2)[:, :, 0, 1:width + 1].transpose(0, 2, 1)
    summed = jnp.zeros(target.shape, jnp.float32)
    for shift_x in (-1, 0, 1):
        for shift_y in (-1, 0, 1):
            entry = (shift_x + 1) * 3 + shift_y + 1
            source = lax.dynamic_slice_in_dim(place, leaf_row + 1 + shift_y, 1, 2)[:, :, 0, 1 + shift_x:1 + shift_x + width].transpose(0, 2, 1)
            charge = lax.dynamic_slice_in_dim(weight, leaf_row + 1 + shift_y, 1, 2)[:, :, 0, 1 + shift_x:1 + shift_x + width].transpose(0, 2, 1)
            present = (lax.dynamic_slice_in_dim(lists[entry], leaf_row, 1, 0)[0] == entry).astype(jnp.float32)
            delta_x = target[0][:, :, None] - (source[0][:, None, :] + shift_x)
            delta_y = target[1][:, :, None] - (source[1][:, None, :] + shift_y)
            delta_z = target[2][:, :, None] - source[2][:, None, :]
            squared = delta_x * delta_x + delta_y * delta_y + delta_z * delta_z
            kernel_row = present[:, None, None] / (FOUR_PI * jnp.sqrt(squared + DELTA_SQ))
            summed = summed + lax.optimization_barrier(jnp.sum(kernel_row[None] * charge[:, :, None, :], axis=-1))
    return summed

def near_field(positions, strengths, ulist):
    grid_x = 2 * SIDE * N_MORTON
    place = jnp.pad(to_grid(positions).astype(jnp.float32), ((0, 0), (0, 0), (1, 1), (1, 1)))
    weight = jnp.pad(to_grid(strengths).astype(jnp.float32), ((0, 0), (0, 0), (1, 1), (1, 1)))
    lists = to_grid(ulist)

    def one_row(leaf_row):
        return row_potential(place, weight, lists, grid_x, leaf_row)
    rows = lax.map(one_row, jnp.arange(2 * SIDE, dtype=jnp.int32))
    return from_grid(rows.transpose(1, 3, 0, 2))

def reference(multipole, positions, strengths, vlist, ulist):
    check = far_field(multipole, vlist)
    potential = near_field(positions, strengths, ulist)
    return (check, potential)
```

```python
import math
from functools import partial

import jax
import jax.numpy as jnp
import ml_dtypes
import numpy as np
from jax import lax
from jax.experimental import pallas as pl
from jax.experimental.pallas import tpu as pltpu
from jax.sharding import PartitionSpec as P

SIDE = 16
EQ_SIDE = 10
FOUR_PI = 4.0 * math.pi
DELTA_SQ = 0.01
RADIUS = 0.525
HALF = 256
WIDE = SIDE + 4
BF16 = jnp.bfloat16
F32 = jnp.float32


def surface_points():
    grid_line = np.linspace(-1.0, 1.0, EQ_SIDE)
    first, second, third = np.meshgrid(grid_line, grid_line, grid_line, indexing="ij")
    stacked = np.stack([first.ravel(), second.ravel(), third.ravel()], axis=1)
    on_face = np.max(np.abs(stacked), axis=1) > 0.999
    return (stacked[on_face] * RADIUS).astype(np.float32)


def translation(points, shift_x, shift_y):
    delta = points[:, None, :] - points[None, :, :]
    ex = delta[..., 0] - np.float32(shift_x)
    ey = delta[..., 1] - np.float32(shift_y)
    ez = delta[..., 2]
    distance = np.sqrt(ex * ex + ey * ey + ez * ez)
    table = (np.float32(1.0) / (np.float32(FOUR_PI) * distance)).astype(ml_dtypes.bfloat16)
    return table.astype(np.float32)


def mirror_halves(points):
    upper = np.nonzero(points[:, 2] > 0)[0]
    mirrored = points[upper] * np.array([1.0, 1.0, -1.0], np.float32)
    gap = np.abs(mirrored[:, None, :] - points[None, :, :]).max(-1)
    lower = gap.argmin(1)
    return upper, lower


def class_offsets(parity_x, parity_y):
    listed = []
    for shift_x in range(-2 - parity_x, 4 - parity_x):
        for shift_y in range(-2 - parity_y, 4 - parity_y):
            if abs(shift_x) > 1 or abs(shift_y) > 1:
                listed.append((shift_x, shift_y))
    return listed


def far_tables():
    points = surface_points()
    upper, lower = mirror_halves(points)
    half, count = len(upper), len(points)
    offsets = [(x, y) for x in range(-3, 4) for y in range(-3, 4) if max(abs(x), abs(y)) > 1]
    weights = np.zeros((len(offsets), 2, HALF, HALF), ml_dtypes.bfloat16)
    for n, (x, y) in enumerate(offsets):
        table = translation(points, x, y)
        same = table[np.ix_(upper, upper)]
        cross = table[np.ix_(upper, lower)]
        weights[n, 0, :half, :half] = (same + cross).T
        weights[n, 1, :half, :half] = (same - cross).T
    fold = np.zeros((count, 2 * HALF), np.float32)
    cols = np.arange(half)
    fold[upper, cols] = 1
    fold[lower, cols] = 1
    fold[upper, HALF + cols] = 1
    fold[lower, HALF + cols] = -1
    unfold = np.concatenate([fold, fold], axis=1) * 0.5
    steps = []
    for n, (x, y) in enumerate(offsets):
        for parity_y in (0, 1):
            for parity_x in (0, 1):
                if (x, y) in class_offsets(parity_x, parity_y):
                    start_x, start_y = 2 + parity_x + x, 2 + parity_y + y
                    steps.append(
                        (n, start_x * 2 + start_y % 2, start_y // 2, parity_y * 2 + parity_x)
                    )
    steps = np.array(steps, np.int32)
    return weights, fold.astype(ml_dtypes.bfloat16), unfold.astype(ml_dtypes.bfloat16), steps


def far_kernel(steps, windows, weights, out, acc):
    acc[...] = jnp.zeros_like(acc)

    def step(n, carry):
        table, window, row, leaf_class = steps[n, 0], steps[n, 1], steps[n, 2], steps[n, 3]
        for e in range(2):
            cols = slice(e * HALF, (e + 1) * HALF)
            source = windows[window, pl.ds(row, 8), :, cols].reshape(256, HALF)
            acc[leaf_class, :, cols] += jnp.dot(
                source, weights[table, e], preferred_element_type=F32
            )
        return carry

    lax.fori_loop(0, steps.shape[0], step, 0, unroll=2)

    def finish(n, carry):
        value = acc[n]
        high = value.astype(BF16)
        out[n, :, : 2 * HALF] = high
        out[n, :, 2 * HALF :] = (value - high.astype(F32)).astype(BF16)
        return carry

    lax.fori_loop(0, 4, finish, 0)


def far_field(windows, weights, steps):
    return pl.pallas_call(
        far_kernel,
        out_shape=jax.ShapeDtypeStruct((4, 256, 4 * HALF), BF16),
        in_specs=[
            pl.BlockSpec(memory_space=pltpu.SMEM),
            pl.BlockSpec(memory_space=pltpu.VMEM),
            pl.BlockSpec(memory_space=pltpu.VMEM),
        ],
        out_specs=pl.BlockSpec(memory_space=pltpu.VMEM),
        scratch_shapes=[pltpu.VMEM((4, 256, 2 * HALF), F32)],
        compiler_params=pltpu.CompilerParams(vmem_limit_bytes=44 * 2**20),
        name="far",
    )(steps, windows, weights)


def near_kernel(target_ref, source_ref, charge_ref, out_ref):
    y = pl.program_id(0)
    leaf = 128
    first_three = lax.broadcasted_iota(jnp.int32, (16, leaf), 0) < 3
    left_half = lax.broadcasted_iota(jnp.int32, (16, 2 * leaf), 1) < leaf
    contract = (((0,), (0,)), ((), ()))

    def pair(i, carry):
        base = pl.multiple_of(i * 2 * leaf, 2 * leaf)
        target = target_ref[y + 1, :, pl.ds(base + leaf, 2 * leaf)]
        nothing = jnp.zeros((16, leaf), BF16)
        split = jnp.concatenate(
            [
                jnp.concatenate([target[:, :leaf], nothing], axis=1),
                jnp.concatenate([nothing, target[:, leaf:]], axis=1),
            ],
            axis=0,
        )
        total = jnp.zeros((16, 2 * leaf), F32)
        for k in range(3):
            source = source_ref[y + k, :, pl.ds(base, 4 * leaf)]
            charge = charge_ref[y + k, :, pl.ds(base, 4 * leaf)]
            middle = lax.dot_general(
                source[:, leaf : 3 * leaf], target, contract, preferred_element_type=F32
            )
            outer = jnp.concatenate([source[:, :leaf], source[:, 3 * leaf :]], axis=0)
            edge = lax.dot_general(outer, split, contract, preferred_element_type=F32)
            total += jnp.dot(
                charge[:, leaf : 3 * leaf],
                lax.rsqrt(middle).astype(BF16),
                preferred_element_type=F32,
            )
            total += jnp.dot(
                jnp.where(first_three, charge[:, :leaf], charge[:, 3 * leaf :]),
                lax.rsqrt(edge).astype(BF16),
                preferred_element_type=F32,
            )
        chosen = jnp.where(left_half, total, pltpu.roll(total, 16 - 3, 0))
        out_ref[0, :, pl.ds(base, 2 * leaf)] = chosen[:8] * (1.0 / FOUR_PI)
        return carry

    lax.fori_loop(0, SIDE // 2, pair, 0, unroll=2)


def near_field(target, source, charge):
    lanes = target.shape[-1]
    whole = pl.BlockSpec((SIDE + 2, 16, lanes), lambda y: (0, 0, 0))
    return pl.pallas_call(
        near_kernel,
        grid=(SIDE,),
        out_shape=jax.ShapeDtypeStruct((SIDE, 8, SIDE * 128), F32),
        in_specs=[whole, whole, whole],
        out_specs=pl.BlockSpec((1, 8, SIDE * 128), lambda y: (y, 0, 0)),
        compiler_params=pltpu.CompilerParams(vmem_limit_bytes=40 * 2**20),
        name="near",
    )(target, source, charge)


def with_halo(square):
    tiles = lax.axis_size("morton")
    quad_y = lax.axis_index("slab") // 2
    sent = jnp.where(quad_y == 0, square[-2:], square[:2])
    other = lax.ppermute(sent, "slab", [(0, 2), (1, 3), (2, 0), (3, 1)])
    blank = jnp.zeros_like(other)
    below = jnp.where(quad_y == 0, blank, other)
    above = jnp.where(quad_y == 0, other, blank)
    tall = jnp.concatenate([below, square, above], axis=0)

    def index(x, y):
        return (x // 2) * 4 + 2 * y + x % 2

    eastward = [(index(x, y), index(x + 1, y)) for x in range(2 * tiles - 1) for y in (0, 1)]
    westward = [(b, a) for a, b in eastward]
    axes = ("morton", "slab")
    west = lax.ppermute(tall[:, -2:], axes, eastward)
    east = lax.ppermute(tall[:, :2], axes, westward)
    return jnp.concatenate([west, tall, east], axis=1)


def near_inputs(places, charges):
    edge = SIDE + 2
    spread = jnp.zeros((edge, edge, 128), F32)
    leaf_x = spread + (jnp.arange(edge, dtype=F32) - 9.0)[None, :, None]
    leaf_y = spread + (jnp.arange(edge, dtype=F32) - 9.0)[:, None, None]
    a0, a1, a2 = (places[:, :, n].astype(F32) for n in range(3))
    square = (a0 + leaf_x) ** 2 + (a1 + leaf_y) ** 2 + a2 * a2
    one = jnp.ones_like(spread)

    def in_three(value):
        high = lax.reduce_precision(value, 8, 7)
        middle = lax.reduce_precision(value - high, 8, 7)
        return [high, middle, value - high - middle]

    nothing = jnp.zeros_like(spread)
    target = [a0, a0, leaf_x, leaf_x, a1, a1, leaf_y, leaf_y, a2]
    target += in_three(square) + [one, one, one, nothing]
    source = [a0, leaf_x, a0, leaf_x, a1, leaf_y, a1, leaf_y, a2]
    source = [-2.0 * s for s in source] + [one, one, one]
    source += in_three(square + DELTA_SQ) + [nothing]

    def stack(parts):
        rows = jnp.stack([p.astype(BF16) for p in parts], axis=1)
        return rows.reshape(edge, 16, edge * 128)

    strength = [charges[:, :, n] for n in range(3)]
    return stack(target), stack(source), stack(strength * 2 + [nothing] * 10)


def body(weights, fold, unfold, steps, multipole, positions, strengths, vlist, ulist):
    del vlist
    eq_count, per_leaf = multipole.shape[1], positions.shape[1]
    occupied = ulist[4] >= 0
    held = occupied.astype(BF16)
    rows = jnp.concatenate(
        [
            (multipole * held).reshape(3 * eq_count, -1),
            positions.reshape(3 * per_leaf, -1),
            (strengths * held).reshape(3 * per_leaf, -1),
        ],
        axis=0,
    )
    square = rows.T.reshape(SIDE, SIDE, -1)
    wide = with_halo(square)
    eq = 3 * eq_count
    folded = jnp.einsum(
        "yxcj,jk->yxck",
        wide[..., :eq].reshape(WIDE, WIDE, 3, eq_count),
        fold,
        preferred_element_type=F32,
    ).astype(BF16)
    folded = jnp.pad(folded, ((0, 0), (0, 0), (0, 1), (0, 0)))
    by_parity = folded.reshape(WIDE // 2, 2, WIDE, 4, 2 * HALF).transpose(1, 0, 2, 3, 4)
    windows = jnp.stack([by_parity[:, :, x : x + SIDE - 1 : 2] for x in range(6)])
    windows = windows.reshape(12, WIDE // 2, 32, 2 * HALF)
    result = far_field(windows, weights, steps)
    result = result.reshape(2, 2, 8, 8, 4, 4 * HALF)[:, :, :, :, :3]
    result = result.transpose(4, 2, 0, 3, 1, 5).reshape(3, SIDE * SIDE, 4 * HALF)
    check = jnp.einsum("clk,ik->cil", result, unfold, preferred_element_type=F32)
    check = check * occupied.astype(F32)
    particles = wide[1:-1, 1:-1, eq:].reshape(SIDE + 2, SIDE + 2, 6, per_leaf)
    target, source, charge = near_inputs(particles[:, :, :3], particles[:, :, 3:])
    potential = near_field(target, source, charge)[:, :3]
    potential = potential.reshape(SIDE, 3, SIDE, per_leaf).transpose(1, 3, 0, 2)
    potential = potential.reshape(3, per_leaf, SIDE * SIDE) * occupied.astype(F32)
    return (check, potential)


def solution(mesh):
    leaves = P(None, None, ("morton", "slab"))
    lists = P(None, ("morton", "slab"))
    whole = [P(), P(), P(), P()]
    tables = far_tables()
    mapped = jax.shard_map(
        body,
        mesh=mesh,
        in_specs=(*whole, leaves, leaves, leaves, lists, lists),
        out_specs=(leaves, leaves),
        check_vma=False,
    )

    def run(multipole, positions, strengths, vlist, ulist):
        return mapped(*(jnp.asarray(t) for t in tables), multipole, positions, strengths, vlist, ulist)

    return run
```

```python
import math

import jax
import jax.numpy as jnp
import ml_dtypes
import numpy as np
from jax import lax
from jax.experimental import pallas as pl
from jax.experimental.pallas import tpu as pltpu
from jax.sharding import PartitionSpec as P

SIDE = 16
EQ_SIDE = 10
FOUR_PI = 4.0 * math.pi
DELTA_SQ = 0.01
RADIUS = 0.525
HALF = 256
WIDE = SIDE + 4
BF16 = jnp.bfloat16
F32 = jnp.float32


def surface_points():
    grid_line = np.linspace(-1.0, 1.0, EQ_SIDE)
    first, second, third = np.meshgrid(grid_line, grid_line, grid_line, indexing="ij")
    stacked = np.stack([first.ravel(), second.ravel(), third.ravel()], axis=1)
    on_face = np.max(np.abs(stacked), axis=1) > 0.999
    return (stacked[on_face] * RADIUS).astype(np.float32)


def translation(points, shift_x, shift_y):
    delta = points[:, None, :] - points[None, :, :]
    ex = delta[..., 0] - np.float32(shift_x)
    ey = delta[..., 1] - np.float32(shift_y)
    ez = delta[..., 2]
    distance = np.sqrt(ex * ex + ey * ey + ez * ez)
    table = (np.float32(1.0) / (np.float32(FOUR_PI) * distance)).astype(ml_dtypes.bfloat16)
    return table.astype(np.float32)


def mirror_halves(points):
    upper = np.nonzero(points[:, 2] > 0)[0]
    mirrored = points[upper] * np.array([1.0, 1.0, -1.0], np.float32)
    gap = np.abs(mirrored[:, None, :] - points[None, :, :]).max(-1)
    lower = gap.argmin(1)
    return upper, lower


def class_offsets(parity_x, parity_y):
    listed = []
    for shift_x in range(-2 - parity_x, 4 - parity_x):
        for shift_y in range(-2 - parity_y, 4 - parity_y):
            if abs(shift_x) > 1 or abs(shift_y) > 1:
                listed.append((shift_x, shift_y))
    return listed


def far_tables():
    points = surface_points()
    upper, lower = mirror_halves(points)
    half, count = len(upper), len(points)
    offsets = [(x, y) for x in range(-3, 4) for y in range(-3, 4) if max(abs(x), abs(y)) > 1]
    weights = np.zeros((len(offsets), 2, HALF, HALF), ml_dtypes.bfloat16)
    for n, (x, y) in enumerate(offsets):
        table = translation(points, x, y)
        same = table[np.ix_(upper, upper)]
        cross = table[np.ix_(upper, lower)]
        weights[n, 0, :half, :half] = (same + cross).T
        weights[n, 1, :half, :half] = (same - cross).T
    fold = np.zeros((count, 2 * HALF), np.float32)
    cols = np.arange(half)
    fold[upper, cols] = 1
    fold[lower, cols] = 1
    fold[upper, HALF + cols] = 1
    fold[lower, HALF + cols] = -1
    unfold = np.concatenate([fold, fold], axis=1) * 0.5
    steps = []
    for n, (x, y) in enumerate(offsets):
        for parity_y in (0, 1):
            for parity_x in (0, 1):
                if (x, y) in class_offsets(parity_x, parity_y):
                    start_x, start_y = 2 + parity_x + x, 2 + parity_y + y
                    steps.append(
                        (n, start_x * 6 + start_y, parity_y * 2 + parity_x)
                    )
    steps = np.array(sorted(steps, key=lambda step: step[2]), np.int32)
    return weights, fold.astype(ml_dtypes.bfloat16), unfold.astype(ml_dtypes.bfloat16), steps


def far_kernel(steps, wide, weights, unfold, occupied, out, rows, windows, sums):
    def widen(y, carry):
        for tile in range(12):
            rows[tile, y] = wide[y, :, tile * 128 : tile * 128 + 128].astype(F32)
        return carry

    lax.fori_loop(0, WIDE, widen, 0)

    def gather(start_y, carry):
        for start_x in range(6):
            for pair in range(4):
                for tile in range(12):
                    first = rows[tile, start_y + 4 * pair, pl.ds(start_x, 8, stride=2), :]
                    second = rows[tile, start_y + 4 * pair + 2, pl.ds(start_x, 8, stride=2), :]
                    at = tile // 4 * 64 + pair * 16
                    cols = slice(tile % 4 * 128, tile % 4 * 128 + 128)
                    windows[start_x * 6 + start_y, at : at + 16, cols] = jnp.concatenate(
                        [first, second], axis=0
                    ).astype(BF16)
        return carry

    lax.fori_loop(0, 6, gather, 0)

    def one_class(n, carry):
        for e in range(2):
            cols = slice(e * HALF, (e + 1) * HALF)
            sources = [windows[steps[n * 27 + k, 1], :, cols] for k in range(27)]
            tables = [weights[steps[n * 27 + k, 0], e] for k in range(27)]
            value = jnp.dot(
                jnp.concatenate(sources, axis=1),
                jnp.concatenate(tables, axis=0),
                preferred_element_type=F32,
            )
            for c in range(3):
                for a in range(8):
                    at = c * 64 + a * 8
                    for b in range(2):
                        sums[
                            e * 2 + b, c * SIDE + 2 * a + n // 2, pl.ds(n % 2, 8, stride=2), :
                        ] = value[at : at + 8, b * 128 : b * 128 + 128]
        return carry

    lax.fori_loop(0, 4, one_class, 0)
    for c in range(3):
        value = jnp.concatenate(
            [sums[n, c * SIDE : (c + 1) * SIDE].reshape(SIDE * SIDE, 128) for n in range(4)],
            axis=1,
        )
        high = value.astype(BF16)
        low = (value - high.astype(F32)).astype(BF16)
        out[c] = (
            lax.dot_general(
                unfold[...],
                jnp.concatenate([high, low], axis=1),
                (((1,), (1,)), ((), ())),
                preferred_element_type=F32,
            )
            * occupied[...]
        )


def far_field(wide, weights, unfold, steps, occupied):
    count = unfold.shape[0]
    vmem = pl.BlockSpec(memory_space=pltpu.VMEM)
    return pl.pallas_call(
        far_kernel,
        out_shape=jax.ShapeDtypeStruct((3, count, SIDE * SIDE), F32),
        in_specs=[pl.BlockSpec(memory_space=pltpu.SMEM), vmem, vmem, vmem, vmem],
        out_specs=vmem,
        scratch_shapes=[
            pltpu.VMEM((12, WIDE, WIDE, 128), F32),
            pltpu.VMEM((36, 192, 2 * HALF), BF16),
            pltpu.VMEM((4, 3 * SIDE, SIDE, 128), F32),
        ],
        compiler_params=pltpu.CompilerParams(vmem_limit_bytes=50 * 2**20),
        name="far",
    )(steps, wide, weights, unfold, occupied)


def near_selection():
    target = [(0, 1), (0, 1), (6, 1), (6, 1), (1, 1), (1, 1), (7, 1), (7, 1), (2, 1)]
    target += [(8, 1), (9, 1), (10, 1), (14, 1), (14, 1), (14, 1), (15, 1)]
    source = [(0, -2), (6, -2), (0, -2), (6, -2), (1, -2), (7, -2), (1, -2), (7, -2), (2, -2)]
    source += [(14, 1), (14, 1), (14, 1), (11, 1), (12, 1), (13, 1), (15, 1)]
    charge = [(3, 1), (4, 1), (5, 1)] * 2 + [(15, 1)] * 10
    table = np.zeros((48, 16), np.float32)
    for row, (column, value) in enumerate(target + source + charge):
        table[row, column] = value
    return table.astype(ml_dtypes.bfloat16)


def near_kernel(select_ref, particle_ref, out_ref, factor_ref):
    y = pl.program_id(0)
    leaf = 128
    first_three = lax.broadcasted_iota(jnp.int32, (16, leaf), 0) < 3
    left_half = lax.broadcasted_iota(jnp.int32, (16, 2 * leaf), 1) < leaf
    contract = (((0,), (0,)), ((), ()))
    lanes = particle_ref.shape[-1]

    @pl.when(y == 0)
    def _():
        line = lax.broadcasted_iota(jnp.int32, (8, lanes), 0)
        column = lax.broadcasted_iota(jnp.int32, (8, lanes), 1) // leaf
        leaf_x = column.astype(F32) - 9.0

        def in_three(value):
            high = value.astype(BF16).astype(F32)
            middle = (value - high).astype(BF16).astype(F32)
            return [high, middle, value - high - middle]

        def factors(row, carry):
            leaf_y = row.astype(F32) - 9.0
            held = particle_ref[row].astype(F32)
            upper = jnp.where(line == 6, leaf_x, jnp.where(line == 7, leaf_y, held))
            place_x = held[0:1] + leaf_x[0:1]
            place_y = held[1:2] + leaf_y
            square = place_x * place_x + place_y * place_y + held[2:3] * held[2:3]
            parts = in_three(square) + in_three(square + DELTA_SQ)
            lower = jnp.where(line == 6, 1.0, 0.0)
            for n, part in enumerate(parts):
                lower = jnp.where(line == n, part, lower)
            base = jnp.concatenate([upper, lower], axis=0).astype(BF16)
            factor_ref[row] = jnp.dot(
                select_ref[...], base, preferred_element_type=F32
            ).astype(BF16)
            return carry

        lax.fori_loop(0, SIDE + 2, factors, 0)

    def pair(i, carry):
        base = pl.multiple_of(i * 2 * leaf, 2 * leaf)
        target = factor_ref[y + 1, 0:16, pl.ds(base + leaf, 2 * leaf)]
        nothing = jnp.zeros((16, leaf), BF16)
        split = jnp.concatenate(
            [
                jnp.concatenate([target[:, :leaf], nothing], axis=1),
                jnp.concatenate([nothing, target[:, leaf:]], axis=1),
            ],
            axis=0,
        )
        inverses, charges = [], []
        for k in range(3):
            source = factor_ref[y + k, 16:32, pl.ds(base, 4 * leaf)]
            charge = factor_ref[y + k, 32:48, pl.ds(base, 4 * leaf)]
            middle = lax.dot_general(
                source[:, leaf : 3 * leaf], target, contract, preferred_element_type=F32
            )
            outer = jnp.concatenate([source[:, :leaf], source[:, 3 * leaf :]], axis=0)
            edge = lax.dot_general(outer, split, contract, preferred_element_type=F32)
            inverses += [lax.rsqrt(middle.astype(BF16)), lax.rsqrt(edge.astype(BF16))]
            charges += [
                charge[:, leaf : 3 * leaf],
                jnp.where(first_three, charge[:, :leaf], charge[:, 3 * leaf :]),
            ]
        total = jnp.dot(
            jnp.concatenate(charges, axis=1),
            jnp.concatenate(inverses, axis=0),
            preferred_element_type=F32,
        )
        chosen = jnp.where(left_half, total, pltpu.roll(total, 16 - 3, 0))
        out_ref[0, :, pl.ds(base, 2 * leaf)] = chosen[:8] * (1.0 / FOUR_PI)
        return carry

    lax.fori_loop(0, SIDE // 2, pair, 0, unroll=4)


def near_field(select, particles):
    lanes = particles.shape[-1]
    return pl.pallas_call(
        near_kernel,
        grid=(SIDE,),
        out_shape=jax.ShapeDtypeStruct((SIDE, 8, SIDE * 128), F32),
        in_specs=[
            pl.BlockSpec((48, 16), lambda y: (0, 0)),
            pl.BlockSpec((SIDE + 2, 8, lanes), lambda y: (0, 0, 0)),
        ],
        out_specs=pl.BlockSpec((1, 8, SIDE * 128), lambda y: (y, 0, 0)),
        scratch_shapes=[pltpu.VMEM((SIDE + 2, 48, lanes), BF16)],
        compiler_params=pltpu.CompilerParams(vmem_limit_bytes=40 * 2**20),
        name="near",
    )(select, particles)


def with_halo(square):
    tiles = lax.axis_size("morton")
    quad_y = lax.axis_index("slab") // 2
    sent = jnp.where(quad_y == 0, square[-2:], square[:2])
    other = lax.ppermute(sent, "slab", [(0, 2), (1, 3), (2, 0), (3, 1)])
    blank = jnp.zeros_like(other)
    below = jnp.where(quad_y == 0, blank, other)
    above = jnp.where(quad_y == 0, other, blank)
    tall = jnp.concatenate([below, square, above], axis=0)

    def index(x, y):
        return (x // 2) * 4 + 2 * y + x % 2

    eastward = [(index(x, y), index(x + 1, y)) for x in range(2 * tiles - 1) for y in (0, 1)]
    westward = [(b, a) for a, b in eastward]
    axes = ("morton", "slab")
    west = lax.ppermute(tall[:, -2:], axes, eastward)
    east = lax.ppermute(tall[:, :2], axes, westward)
    return jnp.concatenate([west, tall, east], axis=1)


def body(weights, fold, unfold, steps, select, multipole, positions, strengths, vlist, ulist):
    del vlist
    per_leaf = positions.shape[1]
    occupied = ulist[4] >= 0
    held = occupied.astype(BF16)
    folded = jnp.einsum(
        "cjl,jk->clk", multipole * held, fold, preferred_element_type=F32
    ).astype(BF16)
    particles = jnp.concatenate([positions, strengths * held], axis=0)
    particles = particles.reshape(6 * per_leaf, -1).T
    square = jnp.concatenate([folded[0], folded[1], folded[2], particles], axis=1)
    wide = with_halo(square.reshape(SIDE, SIDE, -1))
    eq = 6 * HALF
    kept = occupied.astype(F32)
    check = far_field(wide[..., :eq], weights, unfold, steps, kept[None])
    particles = wide[1:-1, 1:-1, eq:].reshape(SIDE + 2, SIDE + 2, 6, per_leaf)
    particles = jnp.pad(particles.transpose(0, 2, 1, 3), ((0, 0), (0, 2), (0, 0), (0, 0)))
    potential = near_field(select, particles.reshape(SIDE + 2, 8, -1))[:, :3]
    potential = potential.reshape(SIDE, 3, SIDE, per_leaf).transpose(1, 3, 0, 2)
    potential = potential.reshape(3, per_leaf, SIDE * SIDE) * kept
    return (check, potential)


def solution(mesh):
    leaves = P(None, None, ("morton", "slab"))
    lists = P(None, ("morton", "slab"))
    whole = [P()] * 5
    tables = (*far_tables(), near_selection())
    mapped = jax.shard_map(
        body,
        mesh=mesh,
        in_specs=(*whole, leaves, leaves, leaves, lists, lists),
        out_specs=(leaves, leaves),
        check_vma=False,
    )

    def run(multipole, positions, strengths, vlist, ulist):
        return mapped(*(jnp.asarray(t) for t in tables), multipole, positions, strengths, vlist, ulist)

    return run
```

```python
import math

import jax
import jax.numpy as jnp
import ml_dtypes
import numpy as np
from jax import lax
from jax.experimental import pallas as pl
from jax.experimental.pallas import tpu as pltpu
from jax.sharding import PartitionSpec as P

SIDE = 16
EQ_SIDE = 10
FOUR_PI = 4.0 * math.pi
DELTA_SQ = 0.01
RADIUS = 0.525
HALF = 256
WIDE = SIDE + 4
BF16 = jnp.bfloat16
F32 = jnp.float32


def surface_points():
    grid_line = np.linspace(-1.0, 1.0, EQ_SIDE)
    first, second, third = np.meshgrid(grid_line, grid_line, grid_line, indexing="ij")
    stacked = np.stack([first.ravel(), second.ravel(), third.ravel()], axis=1)
    on_face = np.max(np.abs(stacked), axis=1) > 0.999
    return (stacked[on_face] * RADIUS).astype(np.float32)


def translation(points, shift_x, shift_y):
    delta = points[:, None, :] - points[None, :, :]
    ex = delta[..., 0] - np.float32(shift_x)
    ey = delta[..., 1] - np.float32(shift_y)
    ez = delta[..., 2]
    distance = np.sqrt(ex * ex + ey * ey + ez * ez)
    table = (np.float32(1.0) / (np.float32(FOUR_PI) * distance)).astype(ml_dtypes.bfloat16)
    return table.astype(np.float32)


def mirror_halves(points):
    upper = np.nonzero(points[:, 2] > 0)[0]
    mirrored = points[upper] * np.array([1.0, 1.0, -1.0], np.float32)
    gap = np.abs(mirrored[:, None, :] - points[None, :, :]).max(-1)
    lower = gap.argmin(1)
    return upper, lower


def class_offsets(parity_x, parity_y):
    listed = []
    for shift_x in range(-2 - parity_x, 4 - parity_x):
        for shift_y in range(-2 - parity_y, 4 - parity_y):
            if abs(shift_x) > 1 or abs(shift_y) > 1:
                listed.append((shift_x, shift_y))
    return listed


def far_tables():
    points = surface_points()
    upper, lower = mirror_halves(points)
    half, count = len(upper), len(points)
    offsets = [(x, y) for x in range(-3, 4) for y in range(-3, 4) if max(abs(x), abs(y)) > 1]
    weights = np.zeros((len(offsets), 2, HALF, HALF), ml_dtypes.bfloat16)
    for n, (x, y) in enumerate(offsets):
        table = translation(points, x, y)
        same = table[np.ix_(upper, upper)]
        cross = table[np.ix_(upper, lower)]
        weights[n, 0, :half, :half] = (same + cross).T
        weights[n, 1, :half, :half] = (same - cross).T
    fold = np.zeros((count, 2 * HALF), np.float32)
    cols = np.arange(half)
    fold[upper, cols] = 1
    fold[lower, cols] = 1
    fold[upper, HALF + cols] = 1
    fold[lower, HALF + cols] = -1
    unfold = np.concatenate([fold, fold], axis=1) * 0.5
    steps = []
    for n, (x, y) in enumerate(offsets):
        for parity_y in (0, 1):
            for parity_x in (0, 1):
                if (x, y) in class_offsets(parity_x, parity_y):
                    start_x, start_y = 2 + parity_x + x, 2 + parity_y + y
                    steps.append(
                        (n, start_x * 6 + start_y, parity_y * 2 + parity_x)
                    )
    steps = np.array(sorted(steps, key=lambda step: step[2]), np.int32)
    return weights, fold.astype(ml_dtypes.bfloat16), unfold.astype(ml_dtypes.bfloat16), steps


def far_kernel(steps, wide, weights, unfold, occupied, out, rows, windows, sums):
    def widen(y, carry):
        for tile in range(12):
            rows[tile, y] = wide[y, :, tile * 128 : tile * 128 + 128].astype(F32)
        return carry

    lax.fori_loop(0, WIDE, widen, 0)

    def gather(start_y, carry):
        for start_x in range(6):
            for pair in range(4):
                for tile in range(12):
                    first = rows[tile, start_y + 4 * pair, pl.ds(start_x, 8, stride=2), :]
                    second = rows[tile, start_y + 4 * pair + 2, pl.ds(start_x, 8, stride=2), :]
                    at = tile // 4 * 64 + pair * 16
                    cols = slice(tile % 4 * 128, tile % 4 * 128 + 128)
                    windows[start_x * 6 + start_y, at : at + 16, cols] = jnp.concatenate(
                        [first, second], axis=0
                    ).astype(BF16)
        return carry

    lax.fori_loop(0, 6, gather, 0)

    def one_class(n, carry):
        for e in range(2):
            cols = slice(e * HALF, (e + 1) * HALF)
            sources = [windows[steps[n * 27 + k, 1], :, cols] for k in range(27)]
            tables = [weights[steps[n * 27 + k, 0], e] for k in range(27)]
            value = jnp.dot(
                jnp.concatenate(sources, axis=1),
                jnp.concatenate(tables, axis=0),
                preferred_element_type=F32,
            )
            for c in range(3):
                for a in range(8):
                    at = c * 64 + a * 8
                    for b in range(2):
                        sums[
                            e * 2 + b, c * SIDE + 2 * a + n // 2, pl.ds(n % 2, 8, stride=2), :
                        ] = value[at : at + 8, b * 128 : b * 128 + 128]
        return carry

    lax.fori_loop(0, 4, one_class, 0)
    for c in range(3):
        value = jnp.concatenate(
            [sums[n, c * SIDE : (c + 1) * SIDE].reshape(SIDE * SIDE, 128) for n in range(4)],
            axis=1,
        )
        high = value.astype(BF16)
        low = (value - high.astype(F32)).astype(BF16)
        out[c] = (
            lax.dot_general(
                unfold[...],
                jnp.concatenate([high, low], axis=1),
                (((1,), (1,)), ((), ())),
                preferred_element_type=F32,
            )
            * occupied[...]
        )


def far_field(wide, weights, unfold, steps, occupied):
    count = unfold.shape[0]
    vmem = pl.BlockSpec(memory_space=pltpu.VMEM)
    return pl.pallas_call(
        far_kernel,
        out_shape=jax.ShapeDtypeStruct((3, count, SIDE * SIDE), F32),
        in_specs=[pl.BlockSpec(memory_space=pltpu.SMEM), vmem, vmem, vmem, vmem],
        out_specs=vmem,
        scratch_shapes=[
            pltpu.VMEM((12, WIDE, WIDE, 128), F32),
            pltpu.VMEM((36, 192, 2 * HALF), BF16),
            pltpu.VMEM((4, 3 * SIDE, SIDE, 128), F32),
        ],
        compiler_params=pltpu.CompilerParams(vmem_limit_bytes=50 * 2**20),
        name="far",
    )(steps, wide, weights, unfold, occupied)


def near_selection():
    target = [(0, 1), (0, 1), (6, 1), (6, 1), (1, 1), (1, 1), (7, 1), (7, 1), (2, 1)]
    target += [(8, 1), (9, 1), (10, 1), (14, 1), (14, 1), (14, 1), (15, 1)]
    source = [(0, -2), (6, -2), (0, -2), (6, -2), (1, -2), (7, -2), (1, -2), (7, -2), (2, -2)]
    source += [(14, 1), (14, 1), (14, 1), (11, 1), (12, 1), (13, 1), (15, 1)]
    charge = [(3, 1), (4, 1), (5, 1)] * 2 + [(15, 1)] * 10
    table = np.zeros((48, 16), np.float32)
    for row, (column, value) in enumerate(target + source + charge):
        table[row, column] = value
    return table.astype(ml_dtypes.bfloat16)


def near_kernel(select_ref, particle_ref, out_ref, factor_ref):
    y = pl.program_id(0)
    leaf = 128
    first_three = lax.broadcasted_iota(jnp.int32, (16, leaf), 0) < 3
    left_half = lax.broadcasted_iota(jnp.int32, (16, 2 * leaf), 1) < leaf
    contract = (((0,), (0,)), ((), ()))
    lanes = particle_ref.shape[-1]

    @pl.when(y == 0)
    def _():
        line = lax.broadcasted_iota(jnp.int32, (8, lanes), 0)
        column = lax.broadcasted_iota(jnp.int32, (8, lanes), 1) // leaf
        leaf_x = column.astype(F32) - 9.0

        def in_three(value):
            high = value.astype(BF16).astype(F32)
            middle = (value - high).astype(BF16).astype(F32)
            return [high, middle, value - high - middle]

        def factors(row, carry):
            leaf_y = row.astype(F32) - 9.0
            held = particle_ref[row].astype(F32)
            upper = jnp.where(line == 6, leaf_x, jnp.where(line == 7, leaf_y, held))
            place_x = held[0:1] + leaf_x[0:1]
            place_y = held[1:2] + leaf_y
            square = place_x * place_x + place_y * place_y + held[2:3] * held[2:3]
            parts = in_three(square) + in_three(square + DELTA_SQ)
            lower = jnp.where(line == 6, 1.0, 0.0)
            for n, part in enumerate(parts):
                lower = jnp.where(line == n, part, lower)
            base = jnp.concatenate([upper, lower], axis=0).astype(BF16)
            factor_ref[row] = jnp.dot(
                select_ref[...], base, preferred_element_type=F32
            ).astype(BF16)
            return carry

        lax.fori_loop(0, SIDE + 2, factors, 0)

    def pair(i, carry):
        base = pl.multiple_of(i * 2 * leaf, 2 * leaf)
        target = factor_ref[y + 1, 0:16, pl.ds(base + leaf, 2 * leaf)]
        nothing = jnp.zeros((16, leaf), BF16)
        split = jnp.concatenate(
            [
                jnp.concatenate([target[:, :leaf], nothing], axis=1),
                jnp.concatenate([nothing, target[:, leaf:]], axis=1),
            ],
            axis=0,
        )
        inverses, charges = [], []
        for k in range(3):
            source = factor_ref[y + k, 16:32, pl.ds(base, 4 * leaf)]
            charge = factor_ref[y + k, 32:48, pl.ds(base, 4 * leaf)]
            middle = lax.dot_general(
                source[:, leaf : 3 * leaf], target, contract, preferred_element_type=F32
            )
            outer = jnp.concatenate([source[:, :leaf], source[:, 3 * leaf :]], axis=0)
            edge = lax.dot_general(outer, split, contract, preferred_element_type=F32)
            inverses += [lax.rsqrt(middle.astype(BF16)), lax.rsqrt(edge.astype(BF16))]
            charges += [
                charge[:, leaf : 3 * leaf],
                jnp.where(first_three, charge[:, :leaf], charge[:, 3 * leaf :]),
            ]
        total = jnp.dot(
            jnp.concatenate(charges, axis=1),
            jnp.concatenate(inverses, axis=0),
            preferred_element_type=F32,
        )
        chosen = jnp.where(left_half, total, pltpu.roll(total, 16 - 3, 0))
        out_ref[0, :, pl.ds(base, 2 * leaf)] = chosen[:8] * (1.0 / FOUR_PI)
        return carry

    lax.fori_loop(0, SIDE // 2, pair, 0, unroll=8)


def near_field(select, particles):
    lanes = particles.shape[-1]
    return pl.pallas_call(
        near_kernel,
        grid=(SIDE,),
        out_shape=jax.ShapeDtypeStruct((SIDE, 8, SIDE * 128), F32),
        in_specs=[
            pl.BlockSpec((48, 16), lambda y: (0, 0)),
            pl.BlockSpec((SIDE + 2, 8, lanes), lambda y: (0, 0, 0)),
        ],
        out_specs=pl.BlockSpec((1, 8, SIDE * 128), lambda y: (y, 0, 0)),
        scratch_shapes=[pltpu.VMEM((SIDE + 2, 48, lanes), BF16)],
        compiler_params=pltpu.CompilerParams(vmem_limit_bytes=40 * 2**20),
        cost_estimate=pl.CostEstimate(
            flops=40_000_000_000, bytes_accessed=2_000_000, transcendentals=0
        ),
        name="near",
    )(select, particles)


def with_halo(square, halo):
    tiles = lax.axis_size("morton")
    quad_y = lax.axis_index("slab") // 2
    sent = jnp.where(quad_y == 0, square[-halo:], square[:halo])
    other = lax.ppermute(sent, "slab", [(0, 2), (1, 3), (2, 0), (3, 1)])
    blank = jnp.zeros_like(other)
    below = jnp.where(quad_y == 0, blank, other)
    above = jnp.where(quad_y == 0, other, blank)
    tall = jnp.concatenate([below, square, above], axis=0)

    def index(x, y):
        return (x // 2) * 4 + 2 * y + x % 2

    eastward = [(index(x, y), index(x + 1, y)) for x in range(2 * tiles - 1) for y in (0, 1)]
    westward = [(b, a) for a, b in eastward]
    axes = ("morton", "slab")
    west = lax.ppermute(tall[:, -halo:], axes, eastward)
    east = lax.ppermute(tall[:, :halo], axes, westward)
    return jnp.concatenate([west, tall, east], axis=1)


def body(weights, fold, unfold, steps, select, multipole, positions, strengths, vlist, ulist):
    del vlist
    per_leaf = positions.shape[1]
    occupied = ulist[4] >= 0
    held = occupied.astype(BF16)
    particles = jnp.concatenate([positions, strengths * held], axis=0)
    particles = particles.reshape(6 * per_leaf, -1).T.reshape(SIDE, SIDE, -1)
    particles = with_halo(particles, 1).reshape(SIDE + 2, SIDE + 2, 6, per_leaf)
    particles = jnp.pad(particles.transpose(0, 2, 1, 3), ((0, 0), (0, 2), (0, 0), (0, 0)))
    folded = jnp.einsum(
        "cjl,jk->clk", multipole * held, fold, preferred_element_type=F32
    ).astype(BF16)
    square = jnp.concatenate([folded[0], folded[1], folded[2]], axis=1)
    wide = with_halo(square.reshape(SIDE, SIDE, -1), 2)
    kept = occupied.astype(F32)
    potential = near_field(select, particles.reshape(SIDE + 2, 8, -1))[:, :3]
    check = far_field(wide, weights, unfold, steps, kept[None])
    potential = potential.reshape(SIDE, 3, SIDE, per_leaf).transpose(1, 3, 0, 2)
    potential = potential.reshape(3, per_leaf, SIDE * SIDE) * kept
    return (check, potential)


def solution(mesh):
    leaves = P(None, None, ("morton", "slab"))
    lists = P(None, ("morton", "slab"))
    whole = [P()] * 5
    tables = (*far_tables(), near_selection())
    mapped = jax.shard_map(
        body,
        mesh=mesh,
        in_specs=(*whole, leaves, leaves, leaves, lists, lists),
        out_specs=(leaves, leaves),
        check_vma=False,
    )

    def run(multipole, positions, strengths, vlist, ulist):
        return mapped(*(jnp.asarray(t) for t in tables), multipole, positions, strengths, vlist, ulist)

    return run
```
